512 devices in a mesh: prompt: 4 (over y_lo, core), seq: 16 (over z), head: 8 (over x, y_hi).
Axes of the slice: x: 4, y: 4 (y_hi: 2, y_lo: 2; y = y_hi * 2 + y_lo), z: 16, core: 2. Of those that a mesh axis runs over, the one named last changes fastest.
Arguments:
- queries: bfloat16 [64, 64, 5120], P(('prompt', 'seq'), None, 'head'), parts along dimension 0, may hold values from -1024 to 1024
- prefix_keys: bfloat16 [262144, 1024], P(('prompt', 'seq'), 'head'), parts along dimension 0, may hold values from -6 to 6
- prefix_values: bfloat16 [262144, 1024], P(('prompt', 'seq'), 'head'), parts along dimension 0, may hold values from -6 to 6
- suffix_keys: bfloat16 [64, 2048, 1024], P(('prompt', 'seq'), None, 'head'), parts along dimension 0, may hold values from -6 to 6
- suffix_values: bfloat16 [64, 2048, 1024], P(('prompt', 'seq'), None, 'head'), parts along dimension 0, may hold values from -6 to 6
- kept_blocks: int32 [64, 64], P('prompt'), parts along dimension 0, may hold values from 0 to 511, as said below
- suffix_lengths: int32 [64], P(('prompt', 'seq')), parts along dimension 0, may hold values from 64 to 2048, as said below
- out_weight: bfloat16 [5120, 5120], P('head', 'seq'), may hold values from -1.75 to 1.75
Outputs:
- projected: float32 [4096, 5120], P(('prompt', 'head'), 'seq'), parts along dimension 0
The draws below stay inside these ranges and needn't reach their ends.
There are 4 independent parts, one for each index of `prompt`. The reference program is written for one: setup_inputs(seed, part) draws one part's arguments, and reference() takes and returns one part's arrays. A program takes and returns all parts, laid end to end along the dimension named above; an argument that names none is the same for every part. Nothing has to cross between parts.
Inputs may be any that keep to these rules, and one draw needn't show every extreme that they name: `kept_blocks`: each row names 64 different prefix blocks. Among the blocks k * 32 to (k + 1) * 32 - 1, for each k, at most 8 are named by one row, and every row names exactly 8 of one such run. `suffix_lengths`: A sample's query tokens are the last 64 of its filled slots; some sample fills all 2048.
All inputs are finite; a program needn't handle non-finite values.
Results may differ from the reference program's by a relative error of at most 0.008.
Values may be sent and summed in bfloat16 or wider, within the bound.
No kernel may reach another device: no remote copies, remote signals or barrier semaphores. Data moves between devices by JAX's collectives and lax.ppermute only.
A program may use at most 64 MiB of HBM per device.

```python
import math
import jax
import jax.numpy as jnp
from jax import lax

D = 5120
HD = 128
GQA = 5
QB = 64
BLOCK = 128
MOST = 8
SUF = 2048
BLK_DEV = 32
KVH = 8
QH = 40
SAMPLES = 16
TOKENS = 1024
NBLK = 512
NTOK = 65536
KEEP = 64
N_SEQ = 16


def key_field(key):
    return jnp.clip(jax.random.normal(jax.random.fold_in(key, 3), (NTOK, KVH * HD), jnp.float32), -6.0, 6.0)


def kept_field(key):
    root = jax.random.fold_in(key, 7)

    def one_sample(sample_key):
        part_a, part_b, part_c, part_d = jax.random.split(sample_key, 4)
        placing = jax.random.permutation(part_a, N_SEQ)
        paired = jax.random.randint(part_b, (N_SEQ // 2,), 0, MOST + 1)
        paired = paired.at[0].set(MOST)
        by_rank = jnp.stack([paired, MOST - paired], axis=1).reshape(N_SEQ)
        counts = jnp.zeros((N_SEQ,), jnp.int32).at[placing].set(by_rank)
        local_order = jax.vmap(lambda inner: jax.random.permutation(inner, BLK_DEV))(jax.random.split(part_c, N_SEQ))
        numbers = jnp.arange(N_SEQ, dtype=jnp.int32)[:, None] * BLK_DEV + local_order.astype(jnp.int32)
        living = jnp.arange(BLK_DEV, dtype=jnp.int32)[None, :] < counts[:, None]
        ranked = jnp.argsort(jnp.where(living, 0, 1).astype(jnp.int32).reshape(-1), stable=True)[:KEEP]
        picked = numbers.reshape(-1)[ranked]
        return jax.random.permutation(part_d, picked)
    return jax.vmap(one_sample)(jax.random.split(root, SAMPLES)).astype(jnp.int32)


def draw_prefix_keys(key, part):
    return key_field(key).astype(jnp.bfloat16)


def draw_kept_blocks(key, part):
    return kept_field(key)


def draw_suffix_lengths(key, part):
    first_key, second_key = jax.random.split(jax.random.fold_in(key, 5))
    lengths = jax.random.randint(first_key, (SAMPLES,), QB, SUF + 1)
    spot = jax.random.randint(second_key, (), 0, SAMPLES)
    return lengths.at[spot].set(SUF).astype(jnp.int32)


def draw_queries(key, part):
    result = 1.5 * jnp.clip(jax.random.normal(jax.random.fold_in(key, 11), (SAMPLES, QB, QH * HD), jnp.float32), -6.0, 6.0)
    return result.astype(jnp.bfloat16)


def steps_of(rng, shape, shards, low, largest):
    loudness, own = 1.0, jax.random.fold_in(rng, 6)
    for position, blocks in shards:
        draws = jnp.exp(jax.random.uniform(jax.random.fold_in(own, position), (blocks,), jnp.float32, low / len(shards), largest / len(shards)))
        loudness = loudness * jnp.repeat(draws, shape[position] // blocks).reshape([-1 if axis == position else 1 for axis in range(len(shape))])
    return loudness


def centred(rng, extent, width, bound, shards=(), kind=jnp.bfloat16):
    drawn = width * jax.random.normal(rng, extent, jnp.float32)
    if shards:
        drawn = drawn * steps_of(rng, extent, shards, -0.22, 0.18)
    return jnp.clip(drawn, -bound, bound).astype(kind)


def setup_inputs(seed: int = 0, part: int = 0) -> dict:
    keys = jax.random.split(jax.random.key(seed), 9)
    part_splits = jax.random.split(jax.random.fold_in(keys[8], part), 9)
    return {
        "queries": draw_queries(jax.random.fold_in(jax.random.fold_in(keys[8], part), 71), part),
        "prefix_keys": draw_prefix_keys(jax.random.fold_in(jax.random.fold_in(keys[8], part), 71), part),
        "prefix_values": centred(part_splits[2], (NTOK, KVH * HD), 1.0, 6.0, ((0, 16), (1, 8))),
        "suffix_keys": centred(part_splits[3], (SAMPLES, SUF, KVH * HD), 1.0, 6.0, ((0, 16), (2, 8))),
        "suffix_values": centred(part_splits[4], (SAMPLES, SUF, KVH * HD), 1.0, 6.0, ((0, 16), (2, 8))),
        "kept_blocks": draw_kept_blocks(jax.random.fold_in(jax.random.fold_in(keys[8], part), 71), part),
        "suffix_lengths": draw_suffix_lengths(jax.random.fold_in(jax.random.fold_in(keys[8], part), 71), part),
        "out_weight": centred(keys[7], (QH * HD, D), (8.0 / D ** 0.5), 1.75, ((0, 8), (1, 16))),
    }


def reference(queries, prefix_keys, prefix_values, suffix_keys, suffix_values, kept_blocks, suffix_lengths, out_weight):
    kv_heads = prefix_keys.shape[1] // HD
    scaling = 1.0 / math.sqrt(HD)
    block_keys = prefix_keys.reshape(NBLK, BLOCK, kv_heads, HD)
    block_values = prefix_values.reshape(NBLK, BLOCK, kv_heads, HD)

    def attend_sample(sample_id):
        kept_ids = kept_blocks[sample_id]
        key_rows = jnp.concatenate([block_keys[kept_ids].reshape(KEEP * BLOCK, kv_heads, HD), suffix_keys[sample_id].reshape(SUF, kv_heads, HD)], 0)
        value_rows = jnp.concatenate([block_values[kept_ids].reshape(KEEP * BLOCK, kv_heads, HD), suffix_values[sample_id].reshape(SUF, kv_heads, HD)], 0)
        asking = queries[sample_id].reshape(QB, kv_heads, GQA, HD)
        scores = jnp.einsum('tgjd,sgd->tgjs', asking.astype(jnp.float32), key_rows.astype(jnp.float32)) * scaling
        slot_pos = jnp.arange(SUF, dtype=jnp.int32)
        last_seen = suffix_lengths[sample_id] - QB + jnp.arange(QB, dtype=jnp.int32)
        own_mask = slot_pos[None, :] <= last_seen[:, None]
        visible = jnp.concatenate([jnp.ones((QB, KEEP * BLOCK), dtype=bool), own_mask], 1)[:, None, None, :]
        maximum = lax.optimization_barrier(jnp.max(jnp.where(visible, scores, -jnp.inf), axis=-1, keepdims=True))
        weights = jnp.where(visible, jnp.exp(scores - maximum), 0.0).astype(jnp.bfloat16)
        weight_sum = lax.optimization_barrier(jnp.sum(weights.astype(jnp.float32), axis=-1))
        summed = jnp.einsum('tgjs,sgd->tgjd', weights.astype(jnp.float32), value_rows.astype(jnp.float32))
        return (summed / weight_sum[..., None]).astype(jnp.bfloat16).reshape(QB, kv_heads * GQA * HD)
    attended = lax.map(attend_sample, jnp.arange(SAMPLES, dtype=jnp.int32)).reshape(TOKENS, -1)
    return jnp.dot(attended, out_weight, preferred_element_type=jnp.float32)
```

```python
import functools
import math

import jax
import jax.numpy as jnp
from jax import lax
from jax.experimental import pallas as pl
from jax.experimental.pallas import tpu as pltpu
from jax.sharding import PartitionSpec as P

HD = 128
GQA = 5
QB = 64
BLOCK = 128
MOST = 8
STEP = 4
ROWS = GQA * QB
FLOOR = -1e30
HIDDEN = -2e30
SCALE2 = math.log2(math.e) / math.sqrt(HD)
WIRE = HD + 16
VMEM_LIMIT = 48 * 2**20


def in_vmem():
    return pl.BlockSpec(memory_space=pltpu.VMEM)


def in_smem():
    return pl.BlockSpec(memory_space=pltpu.SMEM)


def params():
    return pltpu.CompilerParams(vmem_limit_bytes=VMEM_LIMIT)


def slots_kernel(pos_ref, kept_ref, out_ref, *, blocks_here):
    rel = kept_ref[...] - pos_ref[0] * blocks_here
    samples, keep = rel.shape
    lane = lax.broadcasted_iota(jnp.int32, (samples, 128), 1)
    present = jnp.zeros((samples, 128), jnp.int32)
    for i in range(keep):
        present = jnp.where(rel[:, i : i + 1] == lane, 1, present)
    present = jnp.where(lane < blocks_here, present, 0)
    earlier = lax.broadcasted_iota(jnp.int32, (128, 128), 0) < lax.broadcasted_iota(
        jnp.int32, (128, 128), 1
    )
    rank = jnp.dot(
        present.astype(jnp.float32).astype(jnp.bfloat16),
        earlier.astype(jnp.float32).astype(jnp.bfloat16),
        preferred_element_type=jnp.float32,
    ).astype(jnp.int32)
    out = jnp.where(lane == MOST, jnp.sum(present, axis=1, keepdims=True), 0)
    for k in range(MOST):
        chosen = jnp.sum(
            jnp.where((present > 0) & (rank == k), lane, 0), axis=1, keepdims=True
        )
        out = jnp.where(lane == k, chosen, out)
    out_ref[...] = out


def query_rows(q):
    return jnp.concatenate([q[:, j * HD : (j + 1) * HD] for j in range(GQA)], axis=0)


def online_step(carry, scores, values_t):
    top, acc = carry
    new_top = jnp.maximum(top, jnp.max(scores, axis=0, keepdims=True))
    prob = jnp.exp2(scores - new_top).astype(jnp.bfloat16)
    ones = jnp.ones((8, values_t.shape[1]), jnp.bfloat16)
    summed = jnp.dot(
        jnp.concatenate([values_t, ones], axis=0), prob, preferred_element_type=jnp.float32
    )
    return new_top, acc * jnp.exp2(top - new_top) + summed


def start_carry():
    return (
        jnp.full((1, ROWS), FLOOR, jnp.float32),
        jnp.zeros((HD + 8, ROWS), jnp.float32),
    )


def finish(carry):
    top, acc = carry
    total = acc[HD : HD + 1]
    some = total > 0.0
    safe = jnp.where(some, total, 1.0)
    return acc[:HD] / safe, jnp.where(some, top + jnp.log2(safe), FLOOR)


def wire(out, log_sum):
    high = log_sum.astype(jnp.bfloat16)
    rest = log_sum - high.astype(jnp.float32)
    middle = rest.astype(jnp.bfloat16)
    low = (rest - middle.astype(jnp.float32)).astype(jnp.bfloat16)
    row = lax.broadcasted_iota(jnp.int32, (16, out.shape[1]), 0)
    parts = jnp.where(
        row == 0,
        high.astype(jnp.float32),
        jnp.where(row == 1, middle.astype(jnp.float32), low.astype(jnp.float32)),
    )
    return jnp.concatenate([out, parts], axis=0).astype(jnp.bfloat16)


def unwire(packed):
    packed = packed.astype(jnp.float32)
    log_sum = packed[HD : HD + 1] + packed[HD + 1 : HD + 2] + packed[HD + 2 : HD + 3]
    return packed[:HD], log_sum


def merged(parts):
    top = functools.reduce(jnp.maximum, [log_sum for _, log_sum in parts])
    shares = [jnp.exp2(log_sum - top) for _, log_sum in parts]
    total = functools.reduce(jnp.add, shares)
    out = functools.reduce(
        jnp.add, [part * share for (part, _), share in zip(parts, shares, strict=True)]
    )
    return out / total, top + jnp.log2(total)


def prefix_kernel(pos_ref, slots_ref, *refs, offset, classes, ranges):
    q_refs, (k_ref, v_ref, out_ref) = refs[: len(ranges)], refs[len(ranges) :]
    group = lax.rem(pos_ref[0] + offset, classes)
    k = 0
    for q_ref, many in zip(q_refs, ranges, strict=True):
        for i in range(many):
            sample = group + classes * k
            count = slots_ref[sample, MOST]
            asking = query_rows(q_ref[i])

            def step(n, carry, sample=sample, count=count, asking=asking):
                scores, values_t = [], []
                for j in range(STEP):
                    slot = n * STEP + j
                    rows = pl.ds(pl.multiple_of(slots_ref[sample, slot] * BLOCK, BLOCK), BLOCK)
                    found = lax.dot_general(
                        k_ref[rows, :],
                        asking,
                        (((1,), (1,)), ((), ())),
                        preferred_element_type=jnp.float32,
                    )
                    bias = jnp.where(slot < count, 0.0, HIDDEN).astype(jnp.float32)
                    scores.append(found * SCALE2 + bias)
                    values_t.append(v_ref[rows, :].T)
                return online_step(
                    carry, jnp.concatenate(scores, axis=0), jnp.concatenate(values_t, axis=1)
                )

            carry = lax.fori_loop(0, lax.div(count + STEP - 1, STEP), step, start_carry())
            out_ref[:, k * ROWS : (k + 1) * ROWS] = wire(*finish(carry))
            k += 1


def suffix_kernel(length_ref, q_ref, k_ref, v_ref, out_ref):
    chunk = STEP * BLOCK
    asking = query_rows(q_ref[0])
    length = length_ref[0]
    token = lax.rem(lax.broadcasted_iota(jnp.int32, (chunk, ROWS), 1), QB)
    slot = lax.broadcasted_iota(jnp.int32, (chunk, ROWS), 0)

    def step(n, carry):
        rows = pl.ds(pl.multiple_of(n * chunk, chunk), chunk)
        scores = (
            lax.dot_general(
                k_ref[0, rows, :],
                asking,
                (((1,), (1,)), ((), ())),
                preferred_element_type=jnp.float32,
            )
            * SCALE2
        )
        scores = jnp.where(slot - token <= length - QB - n * chunk, scores, HIDDEN)
        return online_step(carry, scores, v_ref[0, rows, :].T)

    carry = lax.fori_loop(0, lax.div(length + chunk - 1, chunk), step, start_carry())
    out, log_sum = finish(carry)
    out_ref[:HD, :] = out
    out_ref[HD:, :] = jnp.broadcast_to(log_sum, (8, ROWS))


def class_kernel(own_ref, before_ref, after_ref, first_ref, second_ref, out_ref, *, members):
    half = first_ref.shape[1]
    for k in range(members):
        lanes = slice(k * ROWS, (k + 1) * ROWS)
        far = first_ref[:, lanes] if k * ROWS < half else second_ref[:, k * ROWS - half : (k + 1) * ROWS - half]
        parts = [
            unwire(x) for x in (own_ref[:, lanes], before_ref[:, lanes], after_ref[:, lanes], far)
        ]
        out_ref[k] = wire(*merged(parts))


def final_kernel(suffix_ref, parts_ref, out_ref):
    parts = [(suffix_ref[:HD, :], suffix_ref[HD : HD + 1, :])]
    parts += [unwire(parts_ref[i]) for i in range(parts_ref.shape[0])]
    out, _ = merged(parts)
    out_ref[0] = out.T.astype(jnp.bfloat16)


def project_kernel(pos_ref, *refs, classes, layout):
    in_refs, (w_ref, out_ref) = refs[: len(layout)], refs[len(layout) :]
    weight = w_ref[...]
    for ref, (offset, first) in zip(in_refs, layout, strict=True):
        group = lax.rem(pos_ref[0] + offset, classes)
        many = ref.shape[0]
        stacked = []
        for i in range(many):
            rows = ref[i]
            stacked.append(
                jnp.concatenate([rows[j * QB : (j + 1) * QB] for j in range(GQA)], axis=1)
            )
        result = jnp.dot(
            jnp.concatenate(stacked, axis=0), weight, preferred_element_type=jnp.float32
        ).astype(jnp.bfloat16)
        for i in range(many):
            sample = group + classes * (first + i)
            out_ref[pl.ds(pl.multiple_of(sample * QB, QB), QB), :] = result[i * QB : (i + 1) * QB]


def shifted(x, distance):
    size = lax.axis_size("seq")
    return lax.ppermute(x, "seq", [((i + distance) % size, i) for i in range(size)])


def body(
    queries,
    prefix_keys,
    prefix_values,
    suffix_keys,
    suffix_values,
    kept_blocks,
    suffix_lengths,
    out_weight,
):
    size, heads = lax.axis_size("seq"), lax.axis_size("head")
    classes = 4
    members = size // classes
    half = members // 2
    groups = [[g + classes * i for i in range(members)] for g in range(classes)]
    position = lax.axis_index("seq").astype(jnp.int32).reshape(1)
    blocks_here = prefix_keys.shape[0] // BLOCK
    bf16, f32 = jnp.bfloat16, jnp.float32

    slots = pl.pallas_call(
        functools.partial(slots_kernel, blocks_here=blocks_here),
        out_shape=jax.ShapeDtypeStruct((kept_blocks.shape[0], 128), jnp.int32),
        in_specs=[in_smem(), in_vmem()],
        out_specs=in_vmem(),
        name="kept_slots",
    )(position, kept_blocks)

    def prefix_part(offset, *asked):
        ranges = tuple(a.shape[0] for a in asked)
        return pl.pallas_call(
            functools.partial(prefix_kernel, offset=offset, classes=classes, ranges=ranges),
            out_shape=jax.ShapeDtypeStruct((WIRE, sum(ranges) * ROWS), bf16),
            in_specs=[in_smem(), in_smem()] + [in_vmem()] * (len(asked) + 2),
            out_specs=in_vmem(),
            compiler_params=params(),
            name="prefix_part",
        )(position, slots, *asked, prefix_keys, prefix_values)

    suffix = pl.pallas_call(
        suffix_kernel,
        out_shape=jax.ShapeDtypeStruct((HD + 8, ROWS), f32),
        in_specs=[in_smem()] + [in_vmem()] * 3,
        out_specs=in_vmem(),
        compiler_params=params(),
        name="suffix_part",
    )(suffix_lengths, queries, suffix_keys, suffix_values)

    mine = lax.all_gather(queries, "seq", axis=0, tiled=True, axis_index_groups=groups)
    from_after = shifted(mine, 1)
    from_before = shifted(mine, -1)
    from_far = (shifted(mine[:half], 2), shifted(mine[half:], -2))

    own = prefix_part(0, mine)
    for_after = prefix_part(1, from_after)
    for_before = prefix_part(3, from_before)
    for_far = prefix_part(2, *from_far)
    cut = half * ROWS
    by_before = shifted(for_after, -1)
    by_after = shifted(for_before, 1)
    by_far = (shifted(for_far[:, :cut], -2), shifted(for_far[:, cut:], 2))

    gathered = pl.pallas_call(
        functools.partial(class_kernel, members=members),
        out_shape=jax.ShapeDtypeStruct((members, WIRE, ROWS), bf16),
        in_specs=[in_vmem()] * 5,
        out_specs=in_vmem(),
        compiler_params=params(),
        name="class_sum",
    )(own, by_before, by_after, *by_far)
    arrived = lax.all_to_all(gathered, "seq", 0, 0, tiled=True, axis_index_groups=groups)
    attended = pl.pallas_call(
        final_kernel,
        out_shape=jax.ShapeDtypeStruct((1, ROWS, HD), bf16),
        in_specs=[in_vmem()] * 2,
        out_specs=in_vmem(),
        compiler_params=params(),
        name="attended",
    )(suffix, arrived)

    same = lax.all_gather(attended, "seq", axis=0, tiled=True, axis_index_groups=groups)
    pieces = [
        (same, (0, 0)),
        (shifted(same, 1), (1, 0)),
        (shifted(same, -1), (3, 0)),
        (shifted(same[:half], 2), (2, 0)),
        (shifted(same[half:], -2), (2, half)),
    ]
    partial_value = pl.pallas_call(
        functools.partial(
            project_kernel, classes=classes, layout=tuple(where for _, where in pieces)
        ),
        out_shape=jax.ShapeDtypeStruct((size * QB, out_weight.shape[1]), bf16),
        in_specs=[in_smem()] + [in_vmem()] * (len(pieces) + 1),
        out_specs=in_vmem(),
        compiler_params=params(),
        name="projection",
    )(position, *[piece for piece, _ in pieces], out_weight)
    sent = lax.all_to_all(
        partial_value.reshape(heads, size * QB // heads, -1), "head", 0, 0, tiled=True
    )
    return jnp.sum(sent.astype(f32), axis=0)


def solution(mesh):
    in_specs = (
        P(("prompt", "seq"), None, "head"),
        P(("prompt", "seq"), "head"),
        P(("prompt", "seq"), "head"),
        P(("prompt", "seq"), None, "head"),
        P(("prompt", "seq"), None, "head"),
        P("prompt", None),
        P(("prompt", "seq")),
        P("head", "seq"),
    )
    out_specs = P(("prompt", "head"), "seq")
    return jax.shard_map(body, mesh=mesh, in_specs=in_specs, out_specs=out_specs, check_vma=False)
```

```python
import functools
import math

import jax
import jax.numpy as jnp
from jax import lax
from jax.experimental import pallas as pl
from jax.experimental.pallas import tpu as pltpu
from jax.sharding import PartitionSpec as P

HD = 128
GQA = 5
QB = 64
BLOCK = 128
MOST = 8
ROWS = GQA * QB
TILE = 128
TOKEN_RUNS = 8
WIDE = 384
FLOOR = -1e30
HIDDEN = -2e30
SCALE2 = math.log2(math.e) / math.sqrt(HD)
WIRE = ROWS + 16
VMEM_LIMIT = 24 * 2**20


def in_vmem():
    return pl.BlockSpec(memory_space=pltpu.VMEM)


def in_smem():
    return pl.BlockSpec(memory_space=pltpu.SMEM)


def params():
    return pltpu.CompilerParams(vmem_limit_bytes=VMEM_LIMIT)


def slots_kernel(pos_ref, kept_ref, out_ref, *, blocks_here):
    rel = kept_ref[...] - pos_ref[0] * blocks_here
    samples, keep = rel.shape
    lane = lax.broadcasted_iota(jnp.int32, (samples, 128), 1)
    present = jnp.zeros((samples, 128), jnp.int32)
    for i in range(keep):
        present = jnp.where(rel[:, i : i + 1] == lane, 1, present)
    present = jnp.where(lane < blocks_here, present, 0)
    earlier = lax.broadcasted_iota(jnp.int32, (128, 128), 0) < lax.broadcasted_iota(
        jnp.int32, (128, 128), 1
    )
    rank = jnp.dot(
        present.astype(jnp.float32).astype(jnp.bfloat16),
        earlier.astype(jnp.float32).astype(jnp.bfloat16),
        preferred_element_type=jnp.float32,
    ).astype(jnp.int32)
    out = jnp.where(lane == MOST, jnp.sum(present, axis=1, keepdims=True), 0)
    for k in range(MOST):
        chosen = jnp.sum(
            jnp.where((present > 0) & (rank == k), lane, 0), axis=1, keepdims=True
        )
        out = jnp.where(lane == k, chosen, out)
    out_ref[...] = out


def query_rows(q):
    return jnp.concatenate([q[:, j * HD : (j + 1) * HD] for j in range(GQA)], axis=0)


def across(asking, keys):
    return (
        lax.dot_general(
            asking, keys, (((1,), (1,)), ((), ())), preferred_element_type=jnp.float32
        )
        * SCALE2
    )


def weighted(prob, values):
    ones = jnp.ones((values.shape[0], HD), jnp.bfloat16)
    return jnp.dot(
        prob, jnp.concatenate([values, ones], axis=1), preferred_element_type=jnp.float32
    )


def laid_flat(stat):
    turned = jnp.concatenate([stat, jnp.zeros((WIDE - ROWS, TILE), jnp.float32)], axis=0).T

    def flat(i):
        row = turned[i : i + 1]
        return jnp.concatenate(
            [row[:, c * TILE : (c + 1) * TILE] for c in range(WIDE // TILE)], axis=0
        )

    return flat


def columns(flats):
    rows = [jnp.concatenate([f[c : c + 1] for c in range(WIDE // TILE)], axis=1) for f in flats]
    spare = -len(rows) % 8
    if spare:
        rows.append(jnp.zeros((spare, WIDE), jnp.float32))
    turned = jnp.concatenate(rows, axis=0).T
    return [turned[:ROWS, i : i + 1] for i in range(len(flats))]


def wire_rows(flat):
    high = flat.astype(jnp.bfloat16).astype(jnp.float32)
    middle = (flat - high).astype(jnp.bfloat16).astype(jnp.float32)
    low = flat - high - middle
    spare = jnp.zeros((WIRE - ROWS - 9, TILE), jnp.float32)
    return jnp.concatenate([high, middle, low, spare], axis=0).astype(jnp.bfloat16)


def unwire_rows(rows):
    rows = rows.astype(jnp.float32)
    return rows[0:3] + rows[3:6] + rows[6:9]


def shares_of(flats):
    top = functools.reduce(jnp.maximum, flats)
    shares = [jnp.exp2(f - top) for f in flats]
    total = functools.reduce(jnp.add, shares)
    return [share / total for share in shares], top + jnp.log2(total)


def added(parts, shares):
    return functools.reduce(
        jnp.add, [p.astype(jnp.float32) * c for p, c in zip(parts, shares, strict=True)]
    )


def prefix_kernel(pos_ref, slots_ref, *refs, offset, classes, ranges):
    n = len(ranges)
    q_refs, k_ref, v_ref, out_refs, stat_ref = refs[:n], refs[n], refs[n + 1], refs[n + 2 : -1], refs[-1]
    group = lax.rem(pos_ref[0] + offset, classes)
    lane = lax.broadcasted_iota(jnp.int32, (ROWS, TILE), 1)
    first = 0
    for q_ref, out_ref, many in zip(q_refs, out_refs, ranges, strict=True):

        def one(i, _, q_ref=q_ref, out_ref=out_ref, first=first):
            sample = group + classes * (first + i)
            count = slots_ref[sample, MOST]

            @pl.when(count == 0)
            def _():
                out_ref[i, :ROWS, :] = jnp.zeros((ROWS, HD), jnp.bfloat16)
                stat_ref[...] = jnp.where(lane == first + i, FLOOR, stat_ref[...])

            for most in range(2, MOST + 1, 2):

                @pl.when((count == most - 1) | (count == most))
                def _(most=most):
                    places = [
                        pl.ds(pl.multiple_of(slots_ref[sample, j] * BLOCK, BLOCK), BLOCK)
                        for j in range(most)
                    ]
                    asking = query_rows(q_ref[i])
                    bias = jnp.where(count == most, 0.0, HIDDEN).astype(jnp.float32)
                    scores = [across(asking, k_ref[place, :]) for place in places]
                    scores[-1] = scores[-1] + bias
                    top = jnp.max(
                        functools.reduce(jnp.maximum, scores), axis=1, keepdims=True
                    )
                    prob = jnp.concatenate(
                        [jnp.exp2(x - top).astype(jnp.bfloat16) for x in scores], axis=1
                    )
                    values = jnp.concatenate([v_ref[place, :] for place in places], axis=0)
                    both = weighted(prob, values)
                    total = both[:, HD:]
                    out_ref[i, :ROWS, :] = (both[:, :HD] / total).astype(jnp.bfloat16)
                    stat_ref[...] = jnp.where(
                        lane == first + i, top + jnp.log2(total), stat_ref[...]
                    )

            return 0

        lax.fori_loop(0, many, one, 0)
        first += many
    flat = laid_flat(stat_ref[...])
    first = 0
    for out_ref, many in zip(out_refs, ranges, strict=True):
        for i in range(many):
            out_ref[i, ROWS:, :] = wire_rows(flat(first + i))
        first += many


def suffix_kernel(length_ref, q_ref, k_ref, v_ref, out_ref):
    chunk = 4 * BLOCK
    asking = query_rows(q_ref[0])
    length = length_ref[0]
    token = lax.rem(lax.broadcasted_iota(jnp.int32, (ROWS, chunk), 0), QB)
    slot = lax.broadcasted_iota(jnp.int32, (ROWS, chunk), 1)

    def step(n, carry):
        top, both = carry
        rows = pl.ds(pl.multiple_of(n * chunk, chunk), chunk)
        scores = across(asking, k_ref[0, rows, :])
        scores = jnp.where(slot - token <= length - QB - n * chunk, scores, HIDDEN)
        new_top = jnp.maximum(top, jnp.max(scores, axis=1, keepdims=True))
        prob = jnp.exp2(scores - new_top).astype(jnp.bfloat16)
        both = both * jnp.exp2(top - new_top) + weighted(prob, v_ref[0, rows, :])
        return new_top, both

    start = (jnp.full((ROWS, 1), FLOOR, jnp.float32), jnp.zeros((ROWS, 2 * HD), jnp.float32))
    top, both = lax.fori_loop(0, lax.div(length + chunk - 1, chunk), step, start)
    total = both[:, HD:]
    out_ref[:ROWS, :] = both[:, :HD] / total
    flat = laid_flat(top + jnp.log2(total))(0)
    out_ref[ROWS:, :] = jnp.concatenate([flat, jnp.zeros((5, TILE), jnp.float32)], axis=0)


def class_kernel(own_ref, before_ref, after_ref, first_ref, second_ref, out_ref, *, members):
    half = first_ref.shape[0]
    parts, shares = [], []
    for k in range(members):
        far_ref, at = (first_ref, k) if k < half else (second_ref, k - half)
        here = [own_ref.at[k], before_ref.at[k], after_ref.at[k], far_ref.at[at]]
        share, log_sum = shares_of([unwire_rows(ref[ROWS:, :]) for ref in here])
        out_ref[k, ROWS:, :] = wire_rows(log_sum)
        parts.append(here)
        shares += share
    shares = columns(shares)
    for k, here in enumerate(parts):
        out_ref[k, :ROWS, :] = added(
            [ref[:ROWS, :] for ref in here], shares[k * len(here) : (k + 1) * len(here)]
        ).astype(jnp.bfloat16)


def final_kernel(suffix_ref, parts_ref, out_ref):
    members = parts_ref.shape[0]
    flats = [suffix_ref[ROWS : ROWS + 3, :]]
    flats += [unwire_rows(parts_ref[i, ROWS:, :]) for i in range(members)]
    shares = columns(shares_of(flats)[0])
    parts = [suffix_ref[:ROWS, :]] + [parts_ref[i, :ROWS, :] for i in range(members)]
    out_ref[0] = added(parts, shares).astype(jnp.bfloat16)


def project_kernel(pos_ref, *refs, classes, layout):
    n = len(layout)
    in_refs, w_ref, out_ref, rows_ref = refs[:n], refs[n], refs[n + 1], refs[n + 2]
    for ref, (offset, first) in zip(in_refs, layout, strict=True):
        group = lax.rem(pos_ref[0] + offset, classes)
        for i in range(ref.shape[0]):
            rows = ref[i]
            sample = group + classes * (first + i)
            rows_ref[pl.ds(pl.multiple_of(sample * QB, QB), QB), :] = jnp.concatenate(
                [rows[j * QB : (j + 1) * QB] for j in range(GQA)], axis=1
            )
    weight = w_ref[...]
    tokens = rows_ref.shape[0] // out_ref.shape[0]
    for i in range(out_ref.shape[0]):
        out_ref[i] = lax.dot_general(
            weight,
            rows_ref[i * tokens : (i + 1) * tokens, :],
            (((1,), (1,)), ((), ())),
            preferred_element_type=jnp.float32,
        ).astype(jnp.bfloat16)


def sum_kernel(parts_ref, out_ref):
    out_ref[...] = functools.reduce(
        jnp.add, [parts_ref[i].astype(jnp.float32) for i in range(parts_ref.shape[0])]
    )


def shifted(x, distance):
    size = lax.axis_size("seq")
    return lax.ppermute(x, "seq", [((i + distance) % size, i) for i in range(size)])


def head_exchange(x):
    return lax.all_to_all(x, "head", 0, 0, tiled=True)


def summed(parts):
    return pl.pallas_call(
        sum_kernel,
        out_shape=jax.ShapeDtypeStruct(parts.shape[1:], jnp.float32),
        in_specs=[in_vmem()],
        out_specs=in_vmem(),
        compiler_params=params(),
        name="head_sum",
    )(parts).T


def body(
    queries,
    prefix_keys,
    prefix_values,
    suffix_keys,
    suffix_values,
    kept_blocks,
    suffix_lengths,
    out_weight,
):
    size = lax.axis_size("seq")
    classes = 4
    members = size // classes
    half = members // 2
    groups = [[g + classes * i for i in range(members)] for g in range(classes)]
    position = lax.axis_index("seq").astype(jnp.int32).reshape(1)
    blocks_here = prefix_keys.shape[0] // BLOCK
    bf16, f32 = jnp.bfloat16, jnp.float32

    slots = pl.pallas_call(
        functools.partial(slots_kernel, blocks_here=blocks_here),
        out_shape=jax.ShapeDtypeStruct((kept_blocks.shape[0], 128), jnp.int32),
        in_specs=[in_smem(), in_vmem()],
        out_specs=in_vmem(),
        name="kept_slots",
    )(position, kept_blocks)

    def prefix_part(offset, *asked):
        ranges = tuple(a.shape[0] for a in asked)
        work = sum(ranges) * ROWS * MOST * BLOCK
        return pl.pallas_call(
            functools.partial(prefix_kernel, offset=offset, classes=classes, ranges=ranges),
            out_shape=[jax.ShapeDtypeStruct((many, WIRE, HD), bf16) for many in ranges],
            in_specs=[in_smem(), in_smem()] + [in_vmem()] * (len(asked) + 2),
            out_specs=[in_vmem()] * len(asked),
            scratch_shapes=[pltpu.VMEM((ROWS, TILE), f32)],
            compiler_params=params(),
            cost_estimate=pl.CostEstimate(
                flops=work * HD * 4, bytes_accessed=2**21, transcendentals=work
            ),
            name="prefix_part",
        )(position, slots, *asked, prefix_keys, prefix_values)

    suffix = pl.pallas_call(
        suffix_kernel,
        out_shape=jax.ShapeDtypeStruct((ROWS + 8, HD), f32),
        in_specs=[in_smem()] + [in_vmem()] * 3,
        out_specs=in_vmem(),
        compiler_params=params(),
        name="suffix_part",
    )(suffix_lengths, queries, suffix_keys, suffix_values)

    def gathered_class(x):
        return lax.all_gather(x, "seq", axis=0, tiled=True, axis_index_groups=groups)

    mine = gathered_class(queries)
    from_after = shifted(mine, 1)
    from_before = shifted(mine, -1)
    from_far = (shifted(mine[:half], 2), shifted(mine[half:], -2))

    (own,) = prefix_part(0, mine)
    (for_after,) = prefix_part(1, from_after)
    (for_before,) = prefix_part(3, from_before)
    for_far = prefix_part(2, *from_far)
    by_before = shifted(for_after, -1)
    by_after = shifted(for_before, 1)
    by_far = (shifted(for_far[0], -2), shifted(for_far[1], 2))

    gathered = pl.pallas_call(
        functools.partial(class_kernel, members=members),
        out_shape=jax.ShapeDtypeStruct((members, WIRE, HD), bf16),
        in_specs=[in_vmem()] * 5,
        out_specs=in_vmem(),
        compiler_params=params(),
        name="class_sum",
    )(own, by_before, by_after, *by_far)
    arrived = lax.all_to_all(gathered, "seq", 0, 0, tiled=True, axis_index_groups=groups)
    attended = pl.pallas_call(
        final_kernel,
        out_shape=jax.ShapeDtypeStruct((1, ROWS, HD), bf16),
        in_specs=[in_vmem()] * 2,
        out_specs=in_vmem(),
        compiler_params=params(),
        name="attended",
    )(suffix, arrived)

    same = gathered_class(attended)
    pieces = [
        (same, (0, 0)),
        (shifted(same, 1), (1, 0)),
        (shifted(same, -1), (3, 0)),
        (shifted(same[:half], 2), (2, 0)),
        (shifted(same[half:], -2), (2, half)),
    ]
    tokens, heads = size * QB, TOKEN_RUNS
    partial_value = pl.pallas_call(
        functools.partial(
            project_kernel, classes=classes, layout=tuple(where for _, where in pieces)
        ),
        out_shape=jax.ShapeDtypeStruct((heads, out_weight.shape[1], tokens // heads), bf16),
        in_specs=[in_smem()] + [in_vmem()] * (len(pieces) + 1),
        out_specs=in_vmem(),
        scratch_shapes=[pltpu.VMEM((tokens, GQA * HD), bf16)],
        compiler_params=params(),
        name="projection",
    )(position, *[piece for piece, _ in pieces], out_weight.T)
    return summed(head_exchange(partial_value))


def solution(mesh):
    in_specs = (
        P(("prompt", "seq"), None, "head"),
        P(("prompt", "seq"), "head"),
        P(("prompt", "seq"), "head"),
        P(("prompt", "seq"), None, "head"),
        P(("prompt", "seq"), None, "head"),
        P("prompt", None),
        P(("prompt", "seq")),
        P("head", "seq"),
    )
    out_specs = P(("prompt", "head"), "seq")
    return jax.shard_map(body, mesh=mesh, in_specs=in_specs, out_specs=out_specs, check_vma=False)
```

```python
import functools
import math

import jax
import jax.numpy as jnp
from jax import lax
from jax.experimental import pallas as pl
from jax.experimental.pallas import tpu as pltpu
from jax.sharding import PartitionSpec as P

HD = 128
GQA = 5
QB = 64
BLOCK = 128
MOST = 8
ROWS = GQA * QB
TILE = 128
TOKEN_RUNS = 8
WIDE = 384
FLOOR = -1e30
HIDDEN = -2e30
SCALE2 = math.log2(math.e) / math.sqrt(HD)
WIRE = ROWS + 16
VMEM_LIMIT = 24 * 2**20


def in_vmem():
    return pl.BlockSpec(memory_space=pltpu.VMEM)


def in_smem():
    return pl.BlockSpec(memory_space=pltpu.SMEM)


def params():
    return pltpu.CompilerParams(vmem_limit_bytes=VMEM_LIMIT)


def group_of(pos_ref, offset, classes):
    return lax.rem(pos_ref[0] + offset * pos_ref[1] + classes, classes)


def slots_of(rel, blocks_here):
    samples, keep = rel.shape
    here = (rel >= 0) & (rel < blocks_here)
    earlier = lax.broadcasted_iota(jnp.int32, (keep, keep), 0) < lax.broadcasted_iota(
        jnp.int32, (keep, keep), 1
    )
    rank = jnp.dot(
        here.astype(jnp.float32).astype(jnp.bfloat16),
        earlier.astype(jnp.float32).astype(jnp.bfloat16),
        preferred_element_type=jnp.float32,
    ).astype(jnp.int32)
    lane = lax.broadcasted_iota(jnp.int32, (samples, 128), 1)
    number = jnp.sum(here.astype(jnp.int32), axis=1, keepdims=True)
    out = jnp.where(lane == MOST, number, 0)
    first = None
    for k in range(MOST):
        chosen = jnp.sum(jnp.where(here & (rank == k), rel, 0), axis=1, keepdims=True)
        if k:
            chosen = jnp.where(number > k, chosen, first)
        else:
            first = chosen
        out = jnp.where(lane == k, chosen, out)
    return out


def query_rows(q):
    return jnp.concatenate([q[:, j * HD : (j + 1) * HD] for j in range(GQA)], axis=0)


def across(asking, keys):
    return (
        lax.dot_general(
            asking, keys, (((1,), (1,)), ((), ())), preferred_element_type=jnp.float32
        )
        * SCALE2
    )


def weighted(prob, values):
    ones = jnp.ones((values.shape[0], HD), jnp.bfloat16)
    return jnp.dot(
        prob, jnp.concatenate([values, ones], axis=1), preferred_element_type=jnp.float32
    )


def laid_flat(stat):
    turned = jnp.concatenate([stat, jnp.zeros((WIDE - ROWS, TILE), jnp.float32)], axis=0).T

    def flat(i):
        row = turned[i : i + 1]
        return jnp.concatenate(
            [row[:, c * TILE : (c + 1) * TILE] for c in range(WIDE // TILE)], axis=0
        )

    return flat


def columns(flats):
    rows = [jnp.concatenate([f[c : c + 1] for c in range(WIDE // TILE)], axis=1) for f in flats]
    spare = -len(rows) % 8
    if spare:
        rows.append(jnp.zeros((spare, WIDE), jnp.float32))
    turned = jnp.concatenate(rows, axis=0).T
    return [turned[:ROWS, i : i + 1] for i in range(len(flats))]


def wire_rows(flat):
    high = flat.astype(jnp.bfloat16).astype(jnp.float32)
    middle = (flat - high).astype(jnp.bfloat16).astype(jnp.float32)
    low = flat - high - middle
    spare = jnp.zeros((WIRE - ROWS - 9, TILE), jnp.float32)
    return jnp.concatenate([high, middle, low, spare], axis=0).astype(jnp.bfloat16)


def unwire_rows(rows):
    rows = rows.astype(jnp.float32)
    return rows[0:3] + rows[3:6] + rows[6:9]


def shares_of(flats):
    top = functools.reduce(jnp.maximum, flats)
    shares = [jnp.exp2(f - top) for f in flats]
    total = functools.reduce(jnp.add, shares)
    return [share / total for share in shares], top + jnp.log2(total)


def added(parts, shares):
    return functools.reduce(
        jnp.add, [p.astype(jnp.float32) * c for p, c in zip(parts, shares, strict=True)]
    )


def attend(group, classes, slots_ref, q_refs, k_ref, v_ref, out_refs):
    ranges = [q_ref.shape[0] for q_ref in q_refs]
    lane = lax.broadcasted_iota(jnp.int32, (ROWS, TILE), 1)
    stat = jnp.zeros((ROWS, TILE), jnp.float32)
    asked = [(q, o, i) for q, o, many in zip(q_refs, out_refs, ranges, strict=True) for i in range(many)]

    def places_of(k):
        return [
            pl.ds(pl.multiple_of(slots_ref[group + classes * k, j] * BLOCK, BLOCK), BLOCK)
            for j in range(MOST)
        ]

    def scores_of(k):
        q_ref, _, i = asked[k]
        asking = query_rows(q_ref[i])
        keys = [k_ref[place, :] for place in places_of(k)]
        return [
            across(asking, jnp.concatenate(keys[j : j + 2], axis=0)) for j in range(0, MOST, 2)
        ]

    coming = scores_of(0)
    for k, (_, out_ref, i) in enumerate(asked):
        scores = coming
        if k + 1 < len(asked):
            coming = scores_of(k + 1)
        count = slots_ref[group + classes * k, MOST]
        top = jnp.max(functools.reduce(jnp.maximum, scores), axis=1, keepdims=True)
        prob = jnp.concatenate([jnp.exp2(x - top).astype(jnp.bfloat16) for x in scores], axis=1)
        used = [(j < count).astype(jnp.float32).astype(jnp.bfloat16) for j in range(MOST)]
        values = jnp.concatenate(
            [
                jnp.concatenate(
                    [v_ref[place, :] * u, jnp.full((BLOCK, HD), u, jnp.bfloat16)], axis=1
                )
                for place, u in zip(places_of(k), used, strict=True)
            ],
            axis=0,
        )
        both = jnp.dot(prob, values, preferred_element_type=jnp.float32)
        total = both[:, HD:]
        some = total > 0.0
        total = jnp.where(some, total, 1.0)
        out_ref[i, :ROWS, :] = (both[:, :HD] / total).astype(jnp.bfloat16)
        stat = jnp.where(lane == k, jnp.where(some, top + jnp.log2(total), FLOOR), stat)
    flat = laid_flat(stat)
    first = 0
    for out_ref, many in zip(out_refs, ranges, strict=True):
        for i in range(many):
            out_ref[i, ROWS:, :] = wire_rows(flat(first + i))
        first += many


def first_kernel(
    pos_ref, kept_ref, q_ref, k_hbm, v_hbm, out_ref, slots_out_ref, k_ref, v_ref, slots_ref, sems, *, offset, classes
):
    k_copy = pltpu.make_async_copy(k_hbm, k_ref, sems.at[0])
    v_copy = pltpu.make_async_copy(v_hbm, v_ref, sems.at[1])
    k_copy.start()
    v_copy.start()
    slots_out_ref[...] = slots_of(kept_ref[...] - pos_ref[0] * (k_ref.shape[0] // BLOCK), k_ref.shape[0] // BLOCK)
    slots_copy = pltpu.make_async_copy(slots_out_ref, slots_ref, sems.at[2])
    slots_copy.start()
    slots_copy.wait()
    k_copy.wait()
    v_copy.wait()
    group = group_of(pos_ref, offset, classes)
    attend(group, classes, slots_ref, [q_ref], k_ref, v_ref, [out_ref])


def prefix_kernel(pos_ref, slots_ref, *refs, offset, classes, many):
    q_refs, k_ref, v_ref, out_refs = refs[:many], refs[many], refs[many + 1], refs[-many:]
    group = group_of(pos_ref, offset, classes)
    attend(group, classes, slots_ref, q_refs, k_ref, v_ref, out_refs)


def suffix_kernel(length_ref, q_ref, k_ref, v_ref, out_ref):
    chunk = 4 * BLOCK
    asking = query_rows(q_ref[0])
    length = length_ref[0]
    token = lax.rem(lax.broadcasted_iota(jnp.int32, (ROWS, chunk), 0), QB)
    slot = lax.broadcasted_iota(jnp.int32, (ROWS, chunk), 1)

    def step(n, carry):
        top, both = carry
        rows = pl.ds(pl.multiple_of(n * chunk, chunk), chunk)
        scores = across(asking, k_ref[0, rows, :])
        scores = jnp.where(slot - token <= length - QB - n * chunk, scores, HIDDEN)
        new_top = jnp.maximum(top, jnp.max(scores, axis=1, keepdims=True))
        prob = jnp.exp2(scores - new_top).astype(jnp.bfloat16)
        both = both * jnp.exp2(top - new_top) + weighted(prob, v_ref[0, rows, :])
        return new_top, both

    start = (jnp.full((ROWS, 1), FLOOR, jnp.float32), jnp.zeros((ROWS, 2 * HD), jnp.float32))
    top, both = lax.fori_loop(0, lax.div(length + chunk - 1, chunk), step, start)
    total = both[:, HD:]
    out_ref[:ROWS, :] = both[:, :HD] / total
    flat = laid_flat(top + jnp.log2(total))(0)
    out_ref[ROWS:, :] = jnp.concatenate([flat, jnp.zeros((5, TILE), jnp.float32)], axis=0)


def class_kernel(own_ref, before_ref, after_ref, far_ref, out_ref, *, members):
    parts, shares = [], []
    for k in range(members):
        here = [ref.at[k] for ref in (own_ref, before_ref, after_ref, far_ref)]
        share, log_sum = shares_of([unwire_rows(ref[ROWS:, :]) for ref in here])
        out_ref[k, ROWS:, :] = wire_rows(log_sum)
        parts.append(here)
        shares += share
    shares = columns(shares)
    for k, here in enumerate(parts):
        out_ref[k, :ROWS, :] = added(
            [ref[:ROWS, :] for ref in here], shares[k * len(here) : (k + 1) * len(here)]
        ).astype(jnp.bfloat16)


def final_kernel(suffix_ref, parts_ref, out_ref):
    members = parts_ref.shape[0]
    flats = [suffix_ref[ROWS : ROWS + 3, :]]
    flats += [unwire_rows(parts_ref[i, ROWS:, :]) for i in range(members)]
    shares = columns(shares_of(flats)[0])
    parts = [suffix_ref[:ROWS, :]] + [parts_ref[i, :ROWS, :] for i in range(members)]
    out_ref[0] = added(parts, shares).astype(jnp.bfloat16)


def put_rows(pos_ref, in_refs, rows_ref, classes, layout):
    for ref, (offset, first) in zip(in_refs, layout, strict=True):
        group = group_of(pos_ref, offset, classes)
        for i in range(ref.shape[0]):
            rows = ref[i]
            sample = group + classes * (first + i)
            rows_ref[pl.ds(pl.multiple_of(sample * QB, QB), QB), :] = jnp.concatenate(
                [rows[j * QB : (j + 1) * QB] for j in range(GQA)], axis=1
            )


def rows_kernel(pos_ref, *refs, classes, layout):
    put_rows(pos_ref, refs[:-1], refs[-1], classes, layout)


def project_kernel(pos_ref, *refs, classes, layout):
    n = len(layout)
    in_refs, w_ref, _, rows_ref, out_ref = refs[:n], *refs[n:]
    put_rows(pos_ref, in_refs, rows_ref, classes, layout)
    weight = w_ref[...]
    tokens = rows_ref.shape[0] // out_ref.shape[0]
    for i in range(out_ref.shape[0]):
        out_ref[i] = lax.dot_general(
            weight,
            rows_ref[i * tokens : (i + 1) * tokens, :],
            (((1,), (1,)), ((), ())),
            preferred_element_type=jnp.float32,
        ).astype(jnp.bfloat16)


def sum_kernel(parts_ref, out_ref):
    out_ref[...] = functools.reduce(
        jnp.add, [parts_ref[i].astype(jnp.float32) for i in range(parts_ref.shape[0])]
    )


def sign_of(prompt):
    return 1 - 2 * (prompt % 2)


def shifted(x, distance):
    prompts, size = lax.axis_size("prompt"), lax.axis_size("seq")
    route = [
        (p * size + (i + distance * sign_of(p)) % size, p * size + i)
        for p in range(prompts)
        for i in range(size)
    ]
    return lax.ppermute(x, ("prompt", "seq"), route)


def head_exchange(x):
    return lax.all_to_all(x, "head", 0, 0, tiled=True)


def summed(parts):
    return pl.pallas_call(
        sum_kernel,
        out_shape=jax.ShapeDtypeStruct(parts.shape[1:], jnp.float32),
        in_specs=[in_vmem()],
        out_specs=in_vmem(),
        compiler_params=params(),
        name="head_sum",
    )(parts).T


def body(
    queries,
    prefix_keys,
    prefix_values,
    suffix_keys,
    suffix_values,
    kept_blocks,
    suffix_lengths,
    out_weight,
):
    size = lax.axis_size("seq")
    classes = 4
    members = size // classes
    groups = [[g + classes * i for i in range(members)] for g in range(classes)]
    position = jnp.stack([lax.axis_index("seq"), sign_of(lax.axis_index("prompt"))]).astype(jnp.int32)
    bf16, f32 = jnp.bfloat16, jnp.float32

    def cost(many):
        work = many * ROWS * MOST * BLOCK
        return pl.CostEstimate(flops=work * HD * 4, bytes_accessed=2**21, transcendentals=work)

    def wired(many):
        return jax.ShapeDtypeStruct((many, WIRE, HD), bf16)

    def first_part(offset, asked):
        anywhere = pl.BlockSpec(memory_space=pltpu.HBM)
        return pl.pallas_call(
            functools.partial(first_kernel, offset=offset, classes=classes),
            out_shape=[
                wired(asked.shape[0]),
                jax.ShapeDtypeStruct((kept_blocks.shape[0], 128), jnp.int32),
                jax.ShapeDtypeStruct(prefix_keys.shape, bf16),
                jax.ShapeDtypeStruct(prefix_values.shape, bf16),
            ],
            in_specs=[in_smem(), in_vmem(), in_vmem(), anywhere, anywhere],
            out_specs=[in_vmem()] * 4,
            scratch_shapes=[
                pltpu.SMEM((kept_blocks.shape[0], 128), jnp.int32),
                pltpu.SemaphoreType.DMA((3,)),
            ],
            compiler_params=params(),
            cost_estimate=cost(asked.shape[0]),
            name="first_part",
        )(position, kept_blocks, asked, prefix_keys, prefix_values)

    def prefix_part(offset, slots, keys, values, *asked):
        return pl.pallas_call(
            functools.partial(prefix_kernel, offset=offset, classes=classes, many=len(asked)),
            out_shape=[wired(a.shape[0]) for a in asked],
            in_specs=[in_smem(), in_smem()] + [in_vmem()] * (len(asked) + 2),
            out_specs=[in_vmem()] * len(asked),
            compiler_params=params(),
            cost_estimate=cost(sum(a.shape[0] for a in asked)),
            name="prefix_part",
        )(position, slots, *asked, keys, values)

    suffix = pl.pallas_call(
        suffix_kernel,
        out_shape=jax.ShapeDtypeStruct((ROWS + 8, HD), f32),
        in_specs=[in_smem()] + [in_vmem()] * 3,
        out_specs=in_vmem(),
        compiler_params=params(),
        name="suffix_part",
    )(suffix_lengths, queries, suffix_keys, suffix_values)

    def gathered_class(x):
        return lax.all_gather(x, "seq", axis=0, tiled=True, axis_index_groups=groups)

    mine = gathered_class(queries)
    from_after = shifted(mine, 1)
    from_before = shifted(mine, -1)
    from_far = shifted(mine, 2)

    for_after, *held = first_part(1, from_after)
    (for_before,) = prefix_part(-1, *held, from_before)
    (for_far,) = prefix_part(2, *held, from_far)
    (own,) = prefix_part(0, *held, mine)
    by_before = shifted(for_after, -1)
    by_after = shifted(for_before, 1)
    by_far = shifted(for_far, -2)

    gathered = pl.pallas_call(
        functools.partial(class_kernel, members=members),
        out_shape=jax.ShapeDtypeStruct((members, WIRE, HD), bf16),
        in_specs=[in_vmem()] * 4,
        out_specs=in_vmem(),
        compiler_params=params(),
        name="class_sum",
    )(own, by_before, by_after, by_far)
    arrived = lax.all_to_all(gathered, "seq", 0, 0, tiled=True, axis_index_groups=groups)
    attended = pl.pallas_call(
        final_kernel,
        out_shape=jax.ShapeDtypeStruct((1, ROWS, HD), bf16),
        in_specs=[in_vmem()] * 2,
        out_specs=in_vmem(),
        compiler_params=params(),
        name="attended",
    )(suffix, arrived)

    same = gathered_class(attended)
    tokens, heads = size * QB, TOKEN_RUNS
    near = ((shifted(same, 1), (1, 0)), (shifted(same, -1), (-1, 0)))
    rest = (
        (same, (0, 0)),
        (shifted(same, 2), (2, 0)),
    )
    rows_shape = jax.ShapeDtypeStruct((tokens, GQA * HD), bf16)
    rows = pl.pallas_call(
        functools.partial(rows_kernel, classes=classes, layout=tuple(w for _, w in rest)),
        out_shape=rows_shape,
        in_specs=[in_smem()] + [in_vmem()] * len(rest),
        out_specs=in_vmem(),
        compiler_params=params(),
        cost_estimate=pl.CostEstimate(flops=3 * 10**10, bytes_accessed=2**21, transcendentals=0),
        name="far_rows",
    )(position, *[piece for piece, _ in rest])
    _, partial_value = pl.pallas_call(
        functools.partial(project_kernel, classes=classes, layout=tuple(w for _, w in near)),
        out_shape=[
            rows_shape,
            jax.ShapeDtypeStruct((heads, out_weight.shape[1], tokens // heads), bf16),
        ],
        in_specs=[in_smem()] + [in_vmem()] * (len(near) + 2),
        out_specs=[in_vmem()] * 2,
        input_output_aliases={len(near) + 2: 0},
        compiler_params=params(),
        name="projection",
    )(position, *[piece for piece, _ in near], out_weight.T, rows)
    return summed(head_exchange(partial_value))


def solution(mesh):
    in_specs = (
        P(("prompt", "seq"), None, "head"),
        P(("prompt", "seq"), "head"),
        P(("prompt", "seq"), "head"),
        P(("prompt", "seq"), None, "head"),
        P(("prompt", "seq"), None, "head"),
        P("prompt", None),
        P(("prompt", "seq")),
        P("head", "seq"),
    )
    out_specs = P(("prompt", "head"), "seq")
    return jax.shard_map(body, mesh=mesh, in_specs=in_specs, out_specs=out_specs, check_vma=False)
```

```python
import functools
import math

import jax
import jax.numpy as jnp
from jax import lax
from jax.experimental import pallas as pl
from jax.experimental.pallas import tpu as pltpu
from jax.sharding import PartitionSpec as P

HD = 128
GQA = 5
QB = 64
BLOCK = 128
MOST = 8
ROWS = GQA * QB
TILE = 128
TOKEN_RUNS = 8
WIDE = 384
FLOOR = -1e30
HIDDEN = -2e30
SCALE2 = math.log2(math.e) / math.sqrt(HD)
WIRE = ROWS + 16
VMEM_LIMIT = 24 * 2**20


def in_vmem():
    return pl.BlockSpec(memory_space=pltpu.VMEM)


def in_smem():
    return pl.BlockSpec(memory_space=pltpu.SMEM)


def params():
    return pltpu.CompilerParams(vmem_limit_bytes=VMEM_LIMIT)


def group_of(pos_ref, offset, classes):
    return lax.rem(pos_ref[0] + offset * pos_ref[1] + classes, classes)


def slots_of(rel, blocks_here):
    samples, keep = rel.shape
    here = (rel >= 0) & (rel < blocks_here)
    earlier = lax.broadcasted_iota(jnp.int32, (keep, keep), 0) < lax.broadcasted_iota(
        jnp.int32, (keep, keep), 1
    )
    rank = jnp.dot(
        here.astype(jnp.float32).astype(jnp.bfloat16),
        earlier.astype(jnp.float32).astype(jnp.bfloat16),
        preferred_element_type=jnp.float32,
    ).astype(jnp.int32)
    lane = lax.broadcasted_iota(jnp.int32, (samples, 128), 1)
    number = jnp.sum(here.astype(jnp.int32), axis=1, keepdims=True)
    out = jnp.where(lane == MOST, number, 0)
    first = None
    for k in range(MOST):
        chosen = jnp.sum(jnp.where(here & (rank == k), rel, 0), axis=1, keepdims=True)
        if k:
            chosen = jnp.where(number > k, chosen, first)
        else:
            first = chosen
        out = jnp.where(lane == k, chosen, out)
    return out


def query_rows(q):
    return jnp.concatenate([q[:, j * HD : (j + 1) * HD] for j in range(GQA)], axis=0)


def across(asking, keys):
    return (
        lax.dot_general(
            asking, keys, (((1,), (1,)), ((), ())), preferred_element_type=jnp.float32
        )
        * SCALE2
    )


def weighted(prob, values):
    ones = jnp.ones((values.shape[0], HD), jnp.bfloat16)
    return jnp.dot(
        prob, jnp.concatenate([values, ones], axis=1), preferred_element_type=jnp.float32
    )


def laid_flat(stat):
    turned = jnp.concatenate([stat, jnp.zeros((WIDE - ROWS, TILE), jnp.float32)], axis=0).T

    def flat(i):
        row = turned[i : i + 1]
        return jnp.concatenate(
            [row[:, c * TILE : (c + 1) * TILE] for c in range(WIDE // TILE)], axis=0
        )

    return flat


def columns(flats):
    rows = [jnp.concatenate([f[c : c + 1] for c in range(WIDE // TILE)], axis=1) for f in flats]
    spare = -len(rows) % 8
    if spare:
        rows.append(jnp.zeros((spare, WIDE), jnp.float32))
    turned = jnp.concatenate(rows, axis=0).T
    return [turned[:ROWS, i : i + 1] for i in range(len(flats))]


def wire_rows(flat):
    high = flat.astype(jnp.bfloat16).astype(jnp.float32)
    middle = (flat - high).astype(jnp.bfloat16).astype(jnp.float32)
    low = flat - high - middle
    spare = jnp.zeros((WIRE - ROWS - 9, TILE), jnp.float32)
    return jnp.concatenate([high, middle, low, spare], axis=0).astype(jnp.bfloat16)


def unwire_rows(rows):
    rows = rows.astype(jnp.float32)
    return rows[0:3] + rows[3:6] + rows[6:9]


def shares_of(flats):
    top = functools.reduce(jnp.maximum, flats)
    shares = [jnp.exp2(f - top) for f in flats]
    total = functools.reduce(jnp.add, shares)
    return [share / total for share in shares], top + jnp.log2(total)


def added(parts, shares):
    return functools.reduce(
        jnp.add, [p.astype(jnp.float32) * c for p, c in zip(parts, shares, strict=True)]
    )


def attend(group, classes, slots_ref, q_refs, k_ref, v_ref, out_refs):
    ranges = [q_ref.shape[0] for q_ref in q_refs]
    lane = lax.broadcasted_iota(jnp.int32, (ROWS, TILE), 1)
    stat = jnp.zeros((ROWS, TILE), jnp.float32)
    asked = [(q, o, i) for q, o, many in zip(q_refs, out_refs, ranges, strict=True) for i in range(many)]

    def places_of(k):
        return [
            pl.ds(pl.multiple_of(slots_ref[group + classes * k, j] * BLOCK, BLOCK), BLOCK)
            for j in range(MOST)
        ]

    def scores_of(k):
        q_ref, _, i = asked[k]
        asking = query_rows(q_ref[i])
        keys = [k_ref[place, :] for place in places_of(k)]
        return [
            across(asking, jnp.concatenate(keys[j : j + 2], axis=0)) for j in range(0, MOST, 2)
        ]

    coming = scores_of(0)
    for k, (_, out_ref, i) in enumerate(asked):
        scores = coming
        if k + 1 < len(asked):
            coming = scores_of(k + 1)
        count = slots_ref[group + classes * k, MOST]
        top = jnp.max(functools.reduce(jnp.maximum, scores), axis=1, keepdims=True)
        prob = jnp.concatenate([jnp.exp2(x - top).astype(jnp.bfloat16) for x in scores], axis=1)
        used = [(j < count).astype(jnp.float32).astype(jnp.bfloat16) for j in range(MOST)]
        values = jnp.concatenate(
            [
                jnp.concatenate(
                    [v_ref[place, :] * u, jnp.full((BLOCK, HD), u, jnp.bfloat16)], axis=1
                )
                for place, u in zip(places_of(k), used, strict=True)
            ],
            axis=0,
        )
        both = jnp.dot(prob, values, preferred_element_type=jnp.float32)
        total = both[:, HD:]
        some = total > 0.0
        total = jnp.where(some, total, 1.0)
        out_ref[i, :ROWS, :] = (both[:, :HD] / total).astype(jnp.bfloat16)
        stat = jnp.where(lane == k, jnp.where(some, top + jnp.log2(total), FLOOR), stat)
    flat = laid_flat(stat)
    first = 0
    for out_ref, many in zip(out_refs, ranges, strict=True):
        for i in range(many):
            out_ref[i, ROWS:, :] = wire_rows(flat(first + i))
        first += many


def first_kernel(
    pos_ref, kept_ref, q_ref, k_hbm, v_hbm, out_ref, slots_out_ref, k_ref, v_ref, slots_ref, sems, *, offset, classes
):
    k_copy = pltpu.make_async_copy(k_hbm, k_ref, sems.at[0])
    v_copy = pltpu.make_async_copy(v_hbm, v_ref, sems.at[1])
    k_copy.start()
    v_copy.start()
    slots_out_ref[...] = slots_of(kept_ref[...] - pos_ref[0] * (k_ref.shape[0] // BLOCK), k_ref.shape[0] // BLOCK)
    slots_copy = pltpu.make_async_copy(slots_out_ref, slots_ref, sems.at[2])
    slots_copy.start()
    slots_copy.wait()
    k_copy.wait()
    v_copy.wait()
    group = group_of(pos_ref, offset, classes)
    attend(group, classes, slots_ref, [q_ref], k_ref, v_ref, [out_ref])


def prefix_kernel(pos_ref, slots_ref, *refs, offset, classes, many):
    q_refs, k_ref, v_ref, out_refs = refs[:many], refs[many], refs[many + 1], refs[-many:]
    group = group_of(pos_ref, offset, classes)
    attend(group, classes, slots_ref, q_refs, k_ref, v_ref, out_refs)


def suffix_kernel(length_ref, q_ref, k_ref, v_ref, out_ref):
    chunk = 4 * BLOCK
    asking = query_rows(q_ref[0])
    length = length_ref[0]
    token = lax.rem(lax.broadcasted_iota(jnp.int32, (ROWS, chunk), 0), QB)
    slot = lax.broadcasted_iota(jnp.int32, (ROWS, chunk), 1)

    def step(n, carry):
        top, both = carry
        rows = pl.ds(pl.multiple_of(n * chunk, chunk), chunk)
        scores = across(asking, k_ref[0, rows, :])
        scores = jnp.where(slot - token <= length - QB - n * chunk, scores, HIDDEN)
        new_top = jnp.maximum(top, jnp.max(scores, axis=1, keepdims=True))
        prob = jnp.exp2(scores - new_top).astype(jnp.bfloat16)
        both = both * jnp.exp2(top - new_top) + weighted(prob, v_ref[0, rows, :])
        return new_top, both

    start = (jnp.full((ROWS, 1), FLOOR, jnp.float32), jnp.zeros((ROWS, 2 * HD), jnp.float32))
    top, both = lax.fori_loop(0, lax.div(length + chunk - 1, chunk), step, start)
    total = both[:, HD:]
    out_ref[:ROWS, :] = both[:, :HD] / total
    flat = laid_flat(top + jnp.log2(total))(0)
    out_ref[ROWS:, :] = jnp.concatenate([flat, jnp.zeros((5, TILE), jnp.float32)], axis=0)


def class_kernel(own_ref, before_ref, after_ref, far_ref, out_ref, *, members):
    parts, shares = [], []
    for k in range(members):
        here = [ref.at[k] for ref in (own_ref, before_ref, after_ref, far_ref)]
        share, log_sum = shares_of([unwire_rows(ref[ROWS:, :]) for ref in here])
        out_ref[k, ROWS:, :] = wire_rows(log_sum)
        parts.append(here)
        shares += share
    shares = columns(shares)
    for k, here in enumerate(parts):
        out_ref[k, :ROWS, :] = added(
            [ref[:ROWS, :] for ref in here], shares[k * len(here) : (k + 1) * len(here)]
        ).astype(jnp.bfloat16)


def final_kernel(suffix_ref, parts_ref, out_ref):
    members = parts_ref.shape[0]
    flats = [suffix_ref[ROWS : ROWS + 3, :]]
    flats += [unwire_rows(parts_ref[i, ROWS:, :]) for i in range(members)]
    shares = columns(shares_of(flats)[0])
    parts = [suffix_ref[:ROWS, :]] + [parts_ref[i, :ROWS, :] for i in range(members)]
    out_ref[0] = added(parts, shares).astype(jnp.bfloat16)


def placed(pos_ref, in_refs, classes, layout):
    for ref, (offset, first) in zip(in_refs, layout, strict=True):
        group = group_of(pos_ref, offset, classes)
        for i in range(ref.shape[0]):
            rows = ref[i]
            yield (
                group + classes * (first + i),
                jnp.concatenate([rows[j * QB : (j + 1) * QB] for j in range(GQA)], axis=1),
            )


def rows_kernel(pos_ref, *refs, classes, layout):
    for sample, rows in placed(pos_ref, refs[:-1], classes, layout):
        refs[-1][lax.div(sample, 2)] = rows


def project_kernel(pos_ref, *refs, classes, layout):
    n = len(layout)
    in_refs, w_ref, done_ref, out_ref, rows_ref = refs[:n], *refs[n:]

    def at(sample):
        return pl.ds(pl.multiple_of(sample * QB, QB), QB)

    own_parity = lax.rem(pos_ref[0], 2)
    for i in range(done_ref.shape[0]):
        rows_ref[at(2 * i + own_parity), :] = done_ref[i]
    for sample, rows in placed(pos_ref, in_refs, classes, layout):
        rows_ref[at(sample), :] = rows
    weight = w_ref[...]
    tokens = rows_ref.shape[0] // out_ref.shape[0]
    for i in range(out_ref.shape[0]):
        out_ref[i] = lax.dot_general(
            weight,
            rows_ref[i * tokens : (i + 1) * tokens, :],
            (((1,), (1,)), ((), ())),
            preferred_element_type=jnp.float32,
        ).astype(jnp.bfloat16)


def sum_kernel(parts_ref, out_ref):
    out_ref[...] = functools.reduce(
        jnp.add, [parts_ref[i].astype(jnp.float32) for i in range(parts_ref.shape[0])]
    )


def sign_of(prompt):
    return 1 - 2 * (prompt % 2)


def shifted(x, distance):
    prompts, size = lax.axis_size("prompt"), lax.axis_size("seq")
    route = [
        (p * size + (i + distance * sign_of(p)) % size, p * size + i)
        for p in range(prompts)
        for i in range(size)
    ]
    return lax.ppermute(x, ("prompt", "seq"), route)


def head_exchange(x):
    return lax.all_to_all(x, "head", 0, 0, tiled=True)


def summed(parts):
    return pl.pallas_call(
        sum_kernel,
        out_shape=jax.ShapeDtypeStruct(parts.shape[1:], jnp.float32),
        in_specs=[in_vmem()],
        out_specs=in_vmem(),
        compiler_params=params(),
        name="head_sum",
    )(parts).T


def body(
    queries,
    prefix_keys,
    prefix_values,
    suffix_keys,
    suffix_values,
    kept_blocks,
    suffix_lengths,
    out_weight,
):
    size = lax.axis_size("seq")
    classes = 4
    members = size // classes
    groups = [[g + classes * i for i in range(members)] for g in range(classes)]
    position = jnp.stack([lax.axis_index("seq"), sign_of(lax.axis_index("prompt"))]).astype(jnp.int32)
    bf16, f32 = jnp.bfloat16, jnp.float32

    def cost(many):
        work = many * ROWS * MOST * BLOCK
        return pl.CostEstimate(flops=work * HD * 4, bytes_accessed=2**21, transcendentals=work)

    def wired(many):
        return jax.ShapeDtypeStruct((many, WIRE, HD), bf16)

    def first_part(offset, asked):
        anywhere = pl.BlockSpec(memory_space=pltpu.HBM)
        return pl.pallas_call(
            functools.partial(first_kernel, offset=offset, classes=classes),
            out_shape=[
                wired(asked.shape[0]),
                jax.ShapeDtypeStruct((kept_blocks.shape[0], 128), jnp.int32),
                jax.ShapeDtypeStruct(prefix_keys.shape, bf16),
                jax.ShapeDtypeStruct(prefix_values.shape, bf16),
            ],
            in_specs=[in_smem(), in_vmem(), in_vmem(), anywhere, anywhere],
            out_specs=[in_vmem()] * 4,
            scratch_shapes=[
                pltpu.SMEM((kept_blocks.shape[0], 128), jnp.int32),
                pltpu.SemaphoreType.DMA((3,)),
            ],
            compiler_params=params(),
            cost_estimate=cost(asked.shape[0]),
            name="first_part",
        )(position, kept_blocks, asked, prefix_keys, prefix_values)

    def prefix_part(offset, slots, keys, values, *asked):
        return pl.pallas_call(
            functools.partial(prefix_kernel, offset=offset, classes=classes, many=len(asked)),
            out_shape=[wired(a.shape[0]) for a in asked],
            in_specs=[in_smem(), in_smem()] + [in_vmem()] * (len(asked) + 2),
            out_specs=[in_vmem()] * len(asked),
            compiler_params=params(),
            cost_estimate=cost(sum(a.shape[0] for a in asked)),
            name="prefix_part",
        )(position, slots, *asked, keys, values)

    suffix = pl.pallas_call(
        suffix_kernel,
        out_shape=jax.ShapeDtypeStruct((ROWS + 8, HD), f32),
        in_specs=[in_smem()] + [in_vmem()] * 3,
        out_specs=in_vmem(),
        compiler_params=params(),
        name="suffix_part",
    )(suffix_lengths, queries, suffix_keys, suffix_values)

    def gathered_class(x):
        return lax.all_gather(x, "seq", axis=0, tiled=True, axis_index_groups=groups)

    mine = gathered_class(queries)
    from_after = shifted(mine, 1)
    from_before = shifted(mine, -1)
    from_far = shifted(mine, 2)

    for_after, *held = first_part(1, from_after)
    (for_before,) = prefix_part(-1, *held, from_before)
    (for_far,) = prefix_part(2, *held, from_far)
    (own,) = prefix_part(0, *held, mine)
    by_before = shifted(for_after, -1)
    by_after = shifted(for_before, 1)
    by_far = shifted(for_far, -2)

    gathered = pl.pallas_call(
        functools.partial(class_kernel, members=members),
        out_shape=jax.ShapeDtypeStruct((members, WIRE, HD), bf16),
        in_specs=[in_vmem()] * 4,
        out_specs=in_vmem(),
        compiler_params=params(),
        name="class_sum",
    )(own, by_before, by_after, by_far)
    arrived = lax.all_to_all(gathered, "seq", 0, 0, tiled=True, axis_index_groups=groups)
    attended = pl.pallas_call(
        final_kernel,
        out_shape=jax.ShapeDtypeStruct((1, ROWS, HD), bf16),
        in_specs=[in_vmem()] * 2,
        out_specs=in_vmem(),
        compiler_params=params(),
        name="attended",
    )(suffix, arrived)

    same = gathered_class(attended)
    tokens, heads = size * QB, TOKEN_RUNS
    near = ((shifted(same, 1), (1, 0)), (shifted(same, -1), (-1, 0)))
    rest = (
        (same, (0, 0)),
        (shifted(same, 2), (2, 0)),
    )
    rows = pl.pallas_call(
        functools.partial(rows_kernel, classes=classes, layout=tuple(w for _, w in rest)),
        out_shape=jax.ShapeDtypeStruct((size // 2, QB, GQA * HD), bf16),
        in_specs=[in_smem()] + [in_vmem()] * len(rest),
        out_specs=in_vmem(),
        compiler_params=params(),
        cost_estimate=pl.CostEstimate(
            flops=3 * 10**10, bytes_accessed=2**21, transcendentals=0
        ),
        name="far_rows",
    )(position, *[piece for piece, _ in rest])
    partial_value = pl.pallas_call(
        functools.partial(project_kernel, classes=classes, layout=tuple(w for _, w in near)),
        out_shape=jax.ShapeDtypeStruct((heads, out_weight.shape[1], tokens // heads), bf16),
        in_specs=[in_smem()] + [in_vmem()] * (len(near) + 2),
        out_specs=in_vmem(),
        scratch_shapes=[pltpu.VMEM((tokens, GQA * HD), bf16)],
        compiler_params=params(),
        name="projection",
    )(position, *[piece for piece, _ in near], out_weight.T, rows)
    return summed(head_exchange(partial_value))


def solution(mesh):
    in_specs = (
        P(("prompt", "seq"), None, "head"),
        P(("prompt", "seq"), "head"),
        P(("prompt", "seq"), "head"),
        P(("prompt", "seq"), None, "head"),
        P(("prompt", "seq"), None, "head"),
        P("prompt", None),
        P(("prompt", "seq")),
        P("head", "seq"),
    )
    out_specs = P(("prompt", "head"), "seq")
    return jax.shard_map(body, mesh=mesh, in_specs=in_specs, out_specs=out_specs, check_vma=False)
```
